1024 devices in a mesh: group: 16 (over x_lo, y), tensor: 64 (over z, x_hi, core).
Axes of the slice: x: 4 (x_hi: 2, x_lo: 2; x = x_hi * 2 + x_lo), y: 8, z: 16, core: 2. Of those that a mesh axis runs over, the one named last changes fastest.
Arguments:
- hidden: bfloat16 [16, 1536, 5120], P('group', 'tensor'), may hold values from -120 to 120
- norm_gain: float32 [5120], replicated, may hold values from 0.5 to 1.5
- cotangent: bfloat16 [2048, 1536], P('tensor'), may hold values from -0.15625 to 0.15625
- master: float32 [2048, 5120], P(('tensor', 'group')), may hold values from -0.078125 to 0.078125
- first_moment: float32 [2048, 5120], P(('tensor', 'group')), may hold values from -1.2 to 1.2
- second_moment: float32 [2048, 5120], P(('tensor', 'group')), may hold values from 0.02 to 0.2
- old_cache: bfloat16 [16, 2048, 1536], P('group', 'tensor'), may hold values from -6 to 6
- stale_pages: int32 [16, 96], P('group'), may hold values 0 or 1
Outputs:
- new_master: float32 [2048, 5120], P(('tensor', 'group'))
- new_first: float32 [2048, 5120], P(('tensor', 'group'))
- new_second: float32 [2048, 5120], P(('tensor', 'group'))
- cache: bfloat16 [16, 2048, 1536], P('group', 'tensor')
The draws below stay inside these ranges and needn't reach their ends.
Inputs may be any that keep to these rules, and one draw needn't show every extreme that they name: `stale_pages`: 1 marks a page of 16 rows whose keys and values are recomputed.
All inputs are finite; a program needn't handle non-finite values. No bound on the sum of `stale_pages` on one device may be relied on, other than what follows from the above.
Results may differ from the reference program's by a relative error of at most 0.0045.
Values may be sent and summed in bfloat16 or wider, within the bound.
A program may use at most 64 MiB of HBM per device.

```python
import math
import jax
import jax.numpy as jnp
from jax import lax

D = 5120
KV_CH = 2048
ROWS = 1536
PAGE = 16
GROUPS = 16
PAGES = 96


def draw_hidden(key, part):
    key = jax.random.fold_in(key, 11)
    key_base, key_rows, key_cols = jax.random.split(key, 3)
    shape = (GROUPS, ROWS, D)
    base = jnp.clip(jax.random.normal(key_base, shape, jnp.float32), -4.0, 4.0)
    row_scale = jnp.exp(jax.random.uniform(key_rows, (GROUPS, ROWS, 1), jnp.float32, 0.0, math.log(10.0)))
    col_scale = jnp.exp(jax.random.uniform(key_cols, (D,), jnp.float32, math.log(0.5), math.log(2.0)))
    return (base * row_scale * col_scale).astype(jnp.bfloat16)


def place_ends(result, stream_key, least, high):
    index_at = [jax.random.randint(jax.random.fold_in(stream_key, axis), (), 0, length) for axis, length in enumerate(result.shape)]
    widest = result.shape.index(max(result.shape))
    next_to = index_at[:widest] + [(index_at[widest] + 1) % result.shape[widest]] + index_at[widest + 1:]
    return result.at[tuple(index_at)].set(least).at[tuple(next_to)].set(high)


def block_levels(rng, extent, cuts, low, largest):
    def one(position, blocks):
        draws = jax.random.uniform(jax.random.fold_in(jax.random.fold_in(rng, 6), position), (blocks,), jnp.float32, low / len(cuts), largest / len(cuts))
        return jnp.repeat(jnp.exp(draws), extent[position] // blocks).reshape((-1,) + (1,) * (len(extent) - position - 1))

    gain = one(*cuts[0])
    for cut in cuts[1:]:
        gain = gain * one(*cut)
    return gain


def centred(own_key, shape, scale, reach, cuts=(), kind=jnp.bfloat16):
    drawn = scale * jax.random.normal(own_key, shape, jnp.float32)
    if cuts:
        drawn = drawn * block_levels(own_key, shape, cuts, -0.22, 0.18)
    return jnp.clip(drawn, -reach, reach).astype(kind)


def setup_inputs(seed: int = 0) -> dict:
    key_list = jax.random.split(jax.random.key(seed), 9)
    return {
        "hidden": draw_hidden(jax.random.fold_in(key_list[8], 71), 0),
        "norm_gain": jnp.clip(1.0 + 0.1 * jax.random.normal(key_list[1], (D,), jnp.float32), 0.5, 1.5),
        "cotangent": centred(key_list[2], (KV_CH, ROWS), ROWS ** -0.5, 0.15625, ((0, 64),)),
        "master": centred(key_list[3], (KV_CH, D), D ** -0.5, 0.078125, ((0, 1024),), jnp.float32),
        "first_moment": centred(key_list[4], (KV_CH, D), 0.2, 1.2, ((0, 1024),), jnp.float32),
        "second_moment": jnp.clip(jnp.exp(math.log(0.2) - 2.3025851 * jax.random.uniform(key_list[5], (KV_CH, D), jnp.float32) ** block_levels(key_list[5], (KV_CH, D), ((0, 1024),), -0.2, 0.2)), 0.02, 0.2),
        "old_cache": centred(key_list[6], (GROUPS, KV_CH, ROWS), 1.0, 6.0, ((0, 16), (1, 64))),
        "stale_pages": place_ends((jax.random.randint(key_list[7], (GROUPS, PAGES), 0, 2) < 1).astype(jnp.int32), jax.random.fold_in(key_list[7], 1), 0, 1),
    }


learning_rate = 0.003
first_decay = 0.9
second_decay = 0.999
adam_epsilon = 1e-08
norm_epsilon = 1e-06
first_correction = 1.0
second_correction = 0.632304575229

def norm_rows(rows_in, norm_gain):
    values = rows_in.astype(jnp.float32)
    inverse = lax.rsqrt(lax.optimization_barrier(jnp.mean(values * values, axis=-1, keepdims=True)) + norm_epsilon)
    return (values * inverse * norm_gain).astype(jnp.bfloat16)

def adam_update(master, first_moment, second_moment, gradient):
    new_first = first_decay * first_moment + (1.0 - first_decay) * gradient
    new_second = second_decay * second_moment + (1.0 - second_decay) * gradient * gradient
    update_step = new_first / first_correction / (jnp.sqrt(new_second / second_correction) + adam_epsilon)
    return (master - learning_rate * update_step, new_first, new_second)

def project(weights, normed_rows):
    return lax.dot_general(weights, normed_rows, (((1,), (1,)), ((), ())), preferred_element_type=jnp.float32)

def reference(hidden, norm_gain, cotangent, master, first_moment, second_moment, old_cache, stale_pages):
    normed = lax.map(lambda rows_in: norm_rows(rows_in, norm_gain), hidden)
    gradient = jnp.dot(cotangent, normed[0], preferred_element_type=jnp.float32)
    new_master, new_first, new_second = adam_update(master, first_moment, second_moment, gradient)
    weights = new_master.astype(jnp.bfloat16)
    recomputed = lax.map(lambda normed_rows: project(weights, normed_rows).astype(jnp.bfloat16), normed)
    page_mask = jnp.repeat(stale_pages, PAGE, axis=-1)
    cache = jnp.where(page_mask[:, None, :] > 0, recomputed, old_cache)
    return (new_master, new_first, new_second, cache)
```

```python
import jax
import jax.numpy as jnp
from jax import lax
from jax.experimental import pallas as pl
from jax.experimental.pallas import tpu as pltpu
from jax.sharding import PartitionSpec as P

PAGE = 16
D = 5120
ROWS = 1536
NZ = 16
NG = 16
DEV_ROWS = 24
CHIP_ROWS = 48
HALF = D // 2
QUARTER = D // 4
SLICE = D // 8
PLANE_CH = 128

learning_rate = 0.003
first_decay = 0.9
second_decay = 0.999
adam_epsilon = 1e-08
norm_epsilon = 1e-06
second_correction = 0.632304575229

MESH = pl.DeviceIdType.MESH
F32 = jnp.float32
BF16 = jnp.bfloat16


def select_matrix(shape, source_of_row):
    row = lax.broadcasted_iota(jnp.int32, shape, 0)
    col = lax.broadcasted_iota(jnp.int32, shape, 1)
    return jnp.where(col == source_of_row(row), 1.0, 0.0).astype(BF16)


def kernel(
    hidden, gain, cot, master, first, second, old, stale,
    new_master, new_first, new_second, cache,
    nsend, ncore, nmine, nbuf, n0, cots, cotp, gsend, grecv, g2send, g2, wsend, w1, wtile, wbuf,
    obuf, o1, osum, o2send, o2,
    core_s, core_r, x_s, x_r, ring_s, ring_r, cot_s, cot_r, l1_s, l1_r, l2_s, l2_r, l3_s, l3_r,
    l5_s, l5_r, l6_s, l6_r, w1_s, w1_r, w2_s, w2_r, o1_s, o1_r, o2_s, o2_r,
):
    g = lax.axis_index("group")
    t = lax.axis_index("tensor")
    xl = g // 8
    y = g % 8
    z = t // 4
    p = t % 4
    xh = p // 2
    co = p % 2

    def dev(group, tensor):
        return (group, tensor)

    def at_z(offset):
        return dev(g, ((z + offset + NZ) % NZ) * 4 + p)

    def at_plane(other):
        return dev(g, z * 4 + other)

    sibling = at_plane(2 * xh + (1 - co))
    partner = at_plane(2 * (1 - xh) + co)

    def copy(src, dst, ss, rs, where):
        return pltpu.make_async_remote_copy(
            src_ref=src, dst_ref=dst, send_sem=ss, recv_sem=rs, device_id=where, device_id_type=MESH
        )

    barrier = pltpu.get_barrier_semaphore()
    greet = [at_z(o) for o in (1, -1, 2, -2, 4, -4, 8)]
    greet += [at_plane((p + k) % 4) for k in (1, 2, 3)]
    greet += [dev((g + k) % NG, t) for k in range(1, NG)]
    for where in greet:
        pl.semaphore_signal(barrier, inc=1, device_id=where, device_id_type=MESH)

    values = hidden[0].astype(F32)
    inverse = lax.rsqrt(jnp.mean(values * values, axis=-1, keepdims=True) + norm_epsilon)
    normed = (values * inverse * gain[...]).astype(BF16)
    for h in range(2):
        nsend[h, 0:DEV_ROWS] = normed[:, h * HALF:(h + 1) * HALF]
        nsend[h, DEV_ROWS:32] = jnp.zeros((8, HALF), BF16)
    ncore[co] = nsend[co]

    pl.semaphore_wait(barrier, len(greet))

    core_out = copy(nsend.at[1 - co], ncore.at[co], core_s, core_r, sibling)
    core_out.start()
    lane = 2 * xl + y // 4
    cot_out = copy(cot, cots.at[p], cot_s, cot_r.at[p], at_plane(lane))

    @pl.when(p != lane)
    def _():
        cot_out.start()

    core_in = copy(nsend.at[1 - co], ncore.at[1 - co], core_s, core_r, sibling)
    core_in.wait_recv()
    for s in range(2):
        for c in range(2):
            nmine[s, c * DEV_ROWS:(c + 1) * DEV_ROWS] = ncore[c, 0:DEV_ROWS, s * QUARTER:(s + 1) * QUARTER]

    def ring(direction, step, chunk):
        sign = 1 if direction == 0 else -1
        slot = (z - sign * step + NZ) % NZ
        row = xh if chunk == 0 else 1 - xh
        src = nbuf.at[slot, row]
        if step == 0 and chunk == 0:
            src = nmine.at[xh]
        return copy(
            src, nbuf.at[slot, row], ring_s.at[direction, step, chunk], ring_r.at[direction, step, chunk],
            at_z(sign),
        )

    def ring_in(direction, step, chunk):
        sign = 1 if direction == 0 else -1
        slot = (z - sign * (step + 1) + NZ) % NZ
        row = xh if chunk == 0 else 1 - xh
        return copy(
            nbuf.at[slot, row], nbuf.at[slot, row], ring_s.at[direction, step, chunk],
            ring_r.at[direction, step, chunk], at_z(-sign),
        )

    def steps(direction, chunk):
        return 8 if direction == chunk else 7

    for d in range(2):
        ring(d, 0, 0).start()
    x_out = copy(nmine.at[1 - xh], nbuf.at[z, xh], x_s, x_r, partner)
    x_out.start()

    def l1(j):
        target = 8 * xh + 4 * co + j
        return copy(
            nmine.at[j // 2, :, (j % 2) * SLICE:(j % 2 + 1) * SLICE], n0.at[z, xh],
            l1_s.at[j], l1_r, dev(target, t),
        )

    for j in range(4):
        @pl.when((g == 0) & ((p != 0) | (j != 0)))
        def _():
            l1(j).start()

    @pl.when((g == 0) & (p == 0))
    def _():
        n0[z, 0] = nmine[0, :, 0:SLICE]

    nbuf[z, xh] = nmine[xh]
    is_lane = p == lane

    @pl.when(is_lane)
    def _():
        for k in range(NZ):
            n0[k, 1 - xl] = jnp.zeros((CHIP_ROWS, SLICE), BF16)
        cots[p] = cot[...]
        for k in range(1, 4):
            other = (p + k) % 4
            copy(cot, cots.at[other], cot_s, cot_r.at[other], at_plane(other)).wait_recv()
        order = select_matrix((PLANE_CH, PLANE_CH), lambda i: ((i // 2) % 4) * 32 + (i // 8) * 2 + i % 2)
        cotp[...] = jnp.dot(
            order, cots[...].reshape(PLANE_CH, ROWS), preferred_element_type=F32
        ).astype(BF16)

    copy(nmine.at[xh], nbuf.at[z, 1 - xh], x_s, x_r, partner).wait_recv()
    for d in range(2):
        ring(d, 0, 1).start()

    def ring_step(step):
        for chunk in range(2):
            for d in range(2):
                if step - 1 < steps(d, chunk):
                    ring_in(d, step - 1, chunk).wait_recv()
                if step < steps(d, chunk):
                    ring(d, step, chunk).start()

    def l2(k):
        return copy(n0.at[z, xl], n0.at[z, xl], l2_s.at[k], l2_r.at[k], at_z(4 * (k + 1)))

    def l2_in(k):
        slot = (z - 4 * (k + 1) + NZ) % NZ
        return copy(n0.at[slot, xl], n0.at[slot, xl], l2_s.at[k], l2_r.at[k], at_z(-4 * (k + 1)))

    n0q = n0.reshape(4, 4, 2, CHIP_ROWS, SLICE)
    hops = ((1, 0, 4), (-1, 0, 4), (2, 0, 2), (-2, 2, 2))

    def l3(k, arriving):
        offset, start, size = hops[k]
        b = (z - offset + NZ) % 4 if arriving else z % 4
        ref = n0q.at[start:start + size, b, xl]
        return copy(ref, ref, l3_s.at[k], l3_r.at[k], at_z(-offset if arriving else offset))

    @pl.when(is_lane)
    def _():
        @pl.when((g != 0) | (p != 0))
        def _():
            copy(n0.at[z, xl], n0.at[z, xl], l1_s.at[0], l1_r, dev((g + 1) % NG, t)).wait_recv()
        for k in range(3):
            l2(k).start()

    ring_step(1)

    @pl.when(is_lane)
    def _():
        for k in range(3):
            l2_in(k).wait_recv()
        for k in range(4):
            l3(k, False).start()

    ring_step(2)

    def l5(k):
        return copy(
            gsend.at[k], grecv.at[y % 4], l5_s.at[k], l5_r.at[y % 4], dev(k, t)
        )

    @pl.when(is_lane)
    def _():
        for k in range(4):
            l3(k, True).wait_recv()
        gsend[...] = jnp.dot(
            cotp[...], n0[...].reshape(ROWS, SLICE), preferred_element_type=F32
        ).reshape(NG, 8, SLICE)
        for k in range(NG):
            @pl.when(g != k)
            def _():
                l5(k).start()
        grecv[y % 4] = gsend[g]

    ring_step(3)

    for j in range(4):
        origin = 8 * xh + 4 * co + j

        @pl.when(g != origin)
        def _():
            copy(gsend.at[0], grecv.at[j], l5_s.at[0], l5_r.at[j], dev(origin, t)).wait_recv()

    for k in range(4):
        for j in range(4):
            g2send[k, j] = grecv[j, 2 * k:2 * k + 2]
    for k in range(1, 4):
        other = (p + k) % 4
        copy(g2send.at[other], g2.at[p], l6_s.at[k - 1], l6_r.at[p], at_plane(other)).start()
    g2[p] = g2send[p]
    for k in range(1, 4):
        other = (p + k) % 4
        copy(g2send.at[p], g2.at[other], l6_s.at[k - 1], l6_r.at[other], at_plane(other)).wait_recv()

    for c in range(2):
        for j in range(4):
            cols = slice((4 * c + j) * SLICE, (4 * c + j + 1) * SLICE)
            gradient = g2[c, j] + g2[2 + c, j]
            m = first_decay * first[:, cols] + (1.0 - first_decay) * gradient
            v = second_decay * second[:, cols] + (1.0 - second_decay) * gradient * gradient
            w = master[:, cols] - learning_rate * (m / (jnp.sqrt(v / second_correction) + adam_epsilon))
            new_first[:, cols] = m
            new_second[:, cols] = v
            new_master[:, cols] = w
            wsend[2 * c + j // 2, :, (j % 2) * SLICE:(j % 2 + 1) * SLICE] = w

    def quarter_of(q):
        return 2 * (q % 2) + q // 2

    for k in range(1, 4):
        other = (p + k) % 4
        copy(wsend.at[quarter_of(other)], w1.at[p], w1_s.at[k - 1], w1_r.at[p], at_plane(other)).start()
    w1[p] = wsend[quarter_of(p)]

    ring_step(4)

    for k in range(1, 4):
        other = (p + k) % 4
        copy(w1.at[other], w1.at[other], w1_s.at[k - 1], w1_r.at[other], at_plane(other)).wait_recv()
    wtile[...] = jnp.concatenate([w1[k] for k in range(4)], axis=0).astype(BF16)
    for k in range(1, NG):
        copy(wtile, wbuf.at[g], w2_s.at[k - 1], w2_r.at[g], dev((g + k) % NG, t)).start()
    wbuf[g] = wtile[...]

    ring_step(5)
    ring_step(6)
    ring_step(7)

    for k in range(1, NG):
        other = (g + k) % NG
        copy(wtile, wbuf.at[other], w2_s.at[k - 1], w2_r.at[other], dev(other, t)).wait_recv()
    back = select_matrix((PLANE_CH, PLANE_CH), lambda c: ((c % 32) // 2) * 8 + (c // 32) * 2 + c % 2)
    weights = jnp.dot(
        back, wbuf[...].astype(F32).reshape(PLANE_CH, QUARTER).astype(BF16), preferred_element_type=F32
    ).astype(BF16)

    ring_step(8)

    for k in range(6):
        rows = slice(256 * k, 256 * (k + 1))
        block = nbuf[...].reshape(ROWS, QUARTER)[rows]
        obuf[:, :, :, rows] = lax.dot_general(
            weights, block, (((1,), (1,)), ((), ())), preferred_element_type=F32
        ).reshape(2, 2, 32, 256)

    o1_out = copy(obuf.at[:, 1 - co], o1, o1_s, o1_r, sibling)
    o1_out.start()
    expand = jnp.where(
        lax.broadcasted_iota(jnp.int32, (ROWS // PAGE, ROWS), 1) // PAGE
        == lax.broadcasted_iota(jnp.int32, (ROWS // PAGE, ROWS), 0),
        1.0, 0.0,
    ).astype(BF16)
    marks = jnp.broadcast_to(stale[...].astype(F32), (8, ROWS // PAGE)).astype(BF16)
    mask = jnp.dot(marks, expand, preferred_element_type=F32)[0:1]
    o1_out.wait_recv()
    for k in range(2):
        osum[k] = obuf[k, co] + o1[k]
    o2send[...] = osum[1 - xh].astype(BF16)
    o2_out = copy(o2send, o2, o2_s, o2_r, partner)
    o2_out.start()
    o2_out.wait_recv()
    result = (osum[xh] + o2[...].astype(F32)).astype(BF16)
    cache[0] = jnp.where(mask > 0.5, result, old[0])

    core_out.wait_send()
    x_out.wait_send()

    @pl.when(p != lane)
    def _():
        cot_out.wait_send()

    for step in range(8):
        for chunk in range(2):
            for d in range(2):
                if step < steps(d, chunk):
                    ring(d, step, chunk).wait_send()
    for j in range(4):
        @pl.when((g == 0) & ((p != 0) | (j != 0)))
        def _():
            l1(j).wait_send()

    @pl.when(is_lane)
    def _():
        for k in range(3):
            l2(k).wait_send()
        for k in range(4):
            l3(k, False).wait_send()
        for k in range(NG):
            @pl.when(g != k)
            def _():
                l5(k).wait_send()

    for k in range(1, 4):
        other = (p + k) % 4
        copy(g2send.at[other], g2.at[p], l6_s.at[k - 1], l6_r.at[p], at_plane(other)).wait_send()
        copy(wsend.at[quarter_of(other)], w1.at[p], w1_s.at[k - 1], w1_r.at[p], at_plane(other)).wait_send()
    for k in range(1, NG):
        copy(wtile, wbuf.at[g], w2_s.at[k - 1], w2_r.at[g], dev((g + k) % NG, t)).wait_send()
    o1_out.wait_send()
    o2_out.wait_send()


def local(hidden, norm_gain, cotangent, master, first_moment, second_moment, old_cache, stale_pages):
    dma = pltpu.SemaphoreType.DMA
    vmem = pl.BlockSpec(memory_space=pltpu.VMEM)
    state = jax.ShapeDtypeStruct((2, D), F32)
    scratch = [
        pltpu.VMEM((2, 32, HALF), BF16),
        pltpu.VMEM((2, 32, HALF), BF16),
        pltpu.VMEM((2, CHIP_ROWS, QUARTER), BF16),
        pltpu.VMEM((NZ, 2, CHIP_ROWS, QUARTER), BF16),
        pltpu.VMEM((NZ, 2, CHIP_ROWS, SLICE), BF16),
        pltpu.VMEM((4, 32, ROWS), BF16),
        pltpu.VMEM((PLANE_CH, ROWS), BF16),
        pltpu.VMEM((NG, 8, SLICE), F32),
        pltpu.VMEM((4, 8, SLICE), F32),
        pltpu.VMEM((4, 4, 2, SLICE), F32),
        pltpu.VMEM((4, 4, 2, SLICE), F32),
        pltpu.VMEM((4, 2, QUARTER), F32),
        pltpu.VMEM((4, 2, QUARTER), F32),
        pltpu.VMEM((8, QUARTER), BF16),
        pltpu.VMEM((NG, 8, QUARTER), BF16),
        pltpu.VMEM((2, 2, 32, ROWS), F32),
        pltpu.VMEM((2, 32, ROWS), F32),
        pltpu.VMEM((2, 32, ROWS), F32),
        pltpu.VMEM((32, ROWS), BF16),
        pltpu.VMEM((32, ROWS), BF16),
        dma, dma, dma, dma, dma((2, 8, 2)), dma((2, 8, 2)), dma, dma((4,)), dma((4,)), dma,
        dma((3,)), dma((3,)), dma((4,)), dma((4,)),
        dma((NG,)), dma((4,)), dma((3,)), dma((4,)), dma((3,)), dma((4,)), dma((NG - 1,)), dma((NG,)),
        dma, dma, dma, dma,
    ]
    return pl.pallas_call(
        kernel,
        out_shape=(state, state, state, jax.ShapeDtypeStruct(old_cache.shape, BF16)),
        in_specs=[vmem] * 8,
        out_specs=(vmem,) * 4,
        scratch_shapes=scratch,
        compiler_params=pltpu.CompilerParams(
            collective_id=0, has_side_effects=True, vmem_limit_bytes=48 * 1024 * 1024
        ),
        cost_estimate=pl.CostEstimate(flops=800_000_000, bytes_accessed=2_000_000, transcendentals=20_000),
    )(
        hidden, norm_gain.reshape(1, D), cotangent, master, first_moment, second_moment, old_cache, stale_pages
    )


def solution(mesh):
    placed = (
        P("group", "tensor", None),
        P(),
        P("tensor", None),
        P(("tensor", "group"), None),
        P(("tensor", "group"), None),
        P(("tensor", "group"), None),
        P("group", "tensor", None),
        P("group", None),
    )
    return jax.shard_map(
        local,
        mesh=mesh,
        in_specs=placed,
        out_specs=(
            P(("tensor", "group"), None),
            P(("tensor", "group"), None),
            P(("tensor", "group"), None),
            P("group", "tensor", None),
        ),
        check_vma=False,
    )
```

```python
import jax
import jax.numpy as jnp
from jax import lax
from jax.experimental import pallas as pl
from jax.experimental.pallas import tpu as pltpu
from jax.sharding import PartitionSpec as P

PAGE = 16
D = 5120
ROWS = 1536
NZ = 16
NG = 16
DEV_ROWS = 24
CHIP_ROWS = 48
HALF = D // 2
QUARTER = D // 4
SLICE = D // 8
WIDTHS = (384, 256)
PLANE_CH = 128

learning_rate = 0.003
first_decay = 0.9
second_decay = 0.999
adam_epsilon = 1e-08
norm_epsilon = 1e-06
second_correction = 0.632304575229

MESH = pl.DeviceIdType.MESH
F32 = jnp.float32
BF16 = jnp.bfloat16


def select_matrix(shape, source_of_row):
    row = lax.broadcasted_iota(jnp.int32, shape, 0)
    col = lax.broadcasted_iota(jnp.int32, shape, 1)
    return jnp.where(col == source_of_row(row), 1.0, 0.0).astype(BF16)


def kernel(
    hidden, gain, cot, master, first, second, old, stale,
    new_master, new_first, new_second, cache,
    hidden_v, gain_v, old_v, stale_v, nsend, ncore, nmine, nbuf, n0, cots, cotp, gsend, grecv, state, newstate,
    wtile, wbuf, obuf, o1, osum, o2send, o2,
    in_s, core_s, core_r, x_s, x_r, ring_s, ring_r, cot_s, cot_r, st_s, st_r, l1_s, l1_r, l2_s, l2_r, l3_s, l3_r,
    l5_s, l5_r, back_s, back_r, w2_s, w2_r, o1_s, o1_r, o2_s, o2_r,
):
    g = lax.axis_index("group")
    t = lax.axis_index("tensor")
    xl = g // 8
    y = g % 8
    z = t // 4
    p = t % 4
    xh = p // 2
    co = p % 2

    def dev(group, tensor):
        return (group, tensor)

    def at_z(offset):
        return dev(g, ((z + offset + NZ) % NZ) * 4 + p)

    def at_plane(other):
        return dev(g, z * 4 + other)

    sibling = at_plane(2 * xh + (1 - co))
    across = 2 * (1 - xh) + co
    partner = at_plane(across)

    def copy(src, dst, ss, rs, where):
        return pltpu.make_async_remote_copy(
            src_ref=src, dst_ref=dst, send_sem=ss, recv_sem=rs, device_id=where, device_id_type=MESH
        )

    barrier = pltpu.get_barrier_semaphore()
    greet = [at_z(o) for o in (1, -1, 2, -2, 4, -4, 8)]
    greet += [at_plane((p + k) % 4) for k in (1, 2, 3)]
    greet += [dev((g + k) % NG, t) for k in range(1, NG)]
    greet += [dev((g + k) % NG, z * 4 + across) for k in range(1, NG)]
    for where in greet:
        pl.semaphore_signal(barrier, inc=1, device_id=where, device_id_type=MESH)

    def quarter_cols(q):
        return pl.ds(pl.multiple_of((2 * (q % 2) + q // 2) * QUARTER, QUARTER), QUARTER)

    lane_of = [2 * w + y // 4 for w in range(2)]
    is_lane = [p == lane_of[w] for w in range(2)]
    any_lane = co == y // 4

    load_hidden = pltpu.make_async_copy(hidden, hidden_v, in_s.at[0])
    load_gain = pltpu.make_async_copy(gain, gain_v, in_s.at[1])
    load_old = pltpu.make_async_copy(old, old_v, in_s.at[2])
    load_stale = pltpu.make_async_copy(stale, stale_v, in_s.at[3])
    load_cot = pltpu.make_async_copy(cot, cots.at[p], cot_r.at[p])
    load_hidden.start()
    load_gain.start()
    load_old.start()
    load_stale.start()
    pl.when(any_lane)(load_cot.start)
    states = (master, first, second)
    load_state = [pltpu.make_async_copy(states[k].at[:, quarter_cols(p)], state.at[k, p], st_r.at[k, p]) for k in range(3)]
    for load in load_state:
        load.start()

    load_hidden.wait()
    load_gain.wait()
    values = hidden_v[0].astype(F32)
    inverse = lax.rsqrt(jnp.mean(values * values, axis=-1, keepdims=True) + norm_epsilon)
    normed = (values * inverse * gain_v[...]).astype(BF16)
    for h in range(2):
        nsend[h, 0:DEV_ROWS] = normed[:, h * HALF:(h + 1) * HALF]
        nsend[h, DEV_ROWS:32] = jnp.zeros((8, HALF), BF16)
    ncore[co] = nsend[co]

    pl.semaphore_wait(barrier, len(greet))

    core_out = copy(nsend.at[1 - co], ncore.at[co], core_s, core_r, sibling)
    core_out.start()

    core_in = copy(nsend.at[1 - co], ncore.at[1 - co], core_s, core_r, sibling)
    core_in.wait_recv()
    for s in range(2):
        for c in range(2):
            nmine[s, c * DEV_ROWS:(c + 1) * DEV_ROWS] = ncore[c, 0:DEV_ROWS, s * QUARTER:(s + 1) * QUARTER]

    def ring(direction, step, chunk):
        sign = 1 if direction == 0 else -1
        slot = (z - sign * step + NZ) % NZ
        row = xh if chunk == 0 else 1 - xh
        src = nbuf.at[slot, row]
        if step == 0 and chunk == 0:
            src = nmine.at[xh]
        return copy(
            src, nbuf.at[slot, row], ring_s.at[direction, step, chunk], ring_r.at[direction, step, chunk],
            at_z(sign),
        )

    def ring_in(direction, step, chunk):
        sign = 1 if direction == 0 else -1
        slot = (z - sign * (step + 1) + NZ) % NZ
        row = xh if chunk == 0 else 1 - xh
        return copy(
            nbuf.at[slot, row], nbuf.at[slot, row], ring_s.at[direction, step, chunk],
            ring_r.at[direction, step, chunk], at_z(-sign),
        )

    def steps(direction, chunk):
        return 8 if direction == chunk else 7

    def l1(j, w):
        target = 8 * xh + 4 * co + j
        start = (j % 2) * SLICE + w * WIDTHS[0]
        return copy(
            nmine.at[j // 2, :, start:start + WIDTHS[w]], n0.at[z, xh, :, 0:WIDTHS[w]],
            l1_s.at[j, w], l1_r, dev(target, z * 4 + 2 * w + co),
        )

    def l1_cond(j, w):
        return (g == 0) & (p != 0) if (j, w) == (0, 0) else g == 0

    for j in range(4):
        for w in range(2):
            pl.when(l1_cond(j, w))(l1(j, w).start)
    x_out = copy(nmine.at[1 - xh], nbuf.at[z, xh], x_s, x_r, partner)
    x_out.start()
    for d in range(2):
        ring(d, 0, 0).start()

    def st(k, i):
        other = (p + i) % 4
        return copy(states[k].at[:, quarter_cols(other)], state.at[k, p], st_s.at[k, i - 1], st_r.at[k, p], at_plane(other))

    def cot_out(w):
        return copy(cot, cots.at[p], cot_s.at[w], cot_r.at[p], at_plane(lane_of[w]))

    for w in range(2):
        pl.when(p != lane_of[w])(cot_out(w).start)
    for i in range(1, 4):
        for k in range(3):
            st(k, i).start()

    @pl.when((g == 0) & (p == 0))
    def _():
        n0[z, 0] = nmine[0, :, 0:WIDTHS[0]]

    nbuf[z, xh] = nmine[xh]

    @pl.when(any_lane)
    def _():
        for k in range(NZ):
            n0[k, 1 - xl] = jnp.zeros((CHIP_ROWS, WIDTHS[0]), BF16)

    @pl.when(is_lane[1])
    def _():
        for k in range(NZ):
            n0[k, xl, :, WIDTHS[1]:WIDTHS[0]] = jnp.zeros((CHIP_ROWS, WIDTHS[0] - WIDTHS[1]), BF16)

    copy(nmine.at[xh], nbuf.at[z, 1 - xh], x_s, x_r, partner).wait_recv()
    for d in range(2):
        ring(d, 0, 1).start()

    def ring_step(step):
        for chunk in range(2):
            for d in range(2):
                if step - 1 < steps(d, chunk):
                    ring_in(d, step - 1, chunk).wait_recv()
                if step < steps(d, chunk):
                    ring(d, step, chunk).start()

    def l2(k, w):
        ref = n0.at[z, xl, :, 0:WIDTHS[w]]
        return copy(ref, ref, l2_s.at[k], l2_r.at[k], at_z(4 * (k + 1)))

    def l2_in(k, w):
        ref = n0.at[(z - 4 * (k + 1) + NZ) % NZ, xl, :, 0:WIDTHS[w]]
        return copy(ref, ref, l2_s.at[k], l2_r.at[k], at_z(-4 * (k + 1)))

    n0q = n0.reshape(4, 4, 2, CHIP_ROWS, WIDTHS[0])
    hops = ((1, 0, 4), (-1, 0, 4), (2, 0, 2), (-2, 2, 2))

    def l3(k, w, arriving):
        offset, start, size = hops[k]
        b = (z - offset + NZ) % 4 if arriving else z % 4
        ref = n0q.at[start:start + size, b, xl, :, 0:WIDTHS[w]]
        return copy(ref, ref, l3_s.at[k], l3_r.at[k], at_z(-offset if arriving else offset))

    for w in range(2):
        @pl.when(is_lane[w])
        def _(w=w):
            @pl.when((g != 0) | (p != 0))
            def _():
                ref = n0.at[z, xl, :, 0:WIDTHS[w]]
                copy(ref, ref, l1_s.at[0, 0], l1_r, dev((g + 1) % NG, t)).wait_recv()
            for k in range(3):
                l2(k, w).start()

    @pl.when(any_lane)
    def _():
        load_cot.wait()
        for k in range(1, 4):
            other = (p + k) % 4
            copy(cot, cots.at[other], cot_s.at[0], cot_r.at[other], at_plane(other)).wait_recv()
        order = select_matrix((PLANE_CH, PLANE_CH), lambda i: ((i // 2) % 4) * 32 + (i // 8) * 2 + i % 2)
        cotp[...] = jnp.dot(
            order, cots[...].reshape(PLANE_CH, ROWS), preferred_element_type=F32
        ).astype(BF16)

    ring_step(1)

    for w in range(2):
        @pl.when(is_lane[w])
        def _(w=w):
            for k in range(3):
                l2_in(k, w).wait_recv()
            for k in range(4):
                l3(k, w, False).start()

    ring_step(2)

    holder = 2 * ((y // 2) % 2) + y // 4

    def l5(k, w):
        return copy(
            gsend.at[k, :, 0:WIDTHS[w]], grecv.at[xl, y % 2, w, :, 0:WIDTHS[w]],
            l5_s.at[k], l5_r.at[xl, y % 2, w], dev(k, z * 4 + holder),
        )

    for w in range(2):
        @pl.when(is_lane[w])
        def _(w=w):
            for k in range(4):
                l3(k, w, True).wait_recv()

    @pl.when(any_lane)
    def _():
        gsend[...] = jnp.dot(
            cotp[...], n0[...].reshape(ROWS, WIDTHS[0]), preferred_element_type=F32
        ).reshape(NG, 8, WIDTHS[0]).astype(BF16)

    for w in range(2):
        @pl.when(is_lane[w])
        def _(w=w):
            for k in range(NG):
                pl.when((g != k) | (p != holder))(l5(k, w).start)

            @pl.when(p == holder)
            def _():
                grecv[xl, y % 2, w] = gsend[g]

    ring_step(3)

    for a in range(2):
        for j in range(2):
            for w in range(2):
                origin = 8 * a + 4 * co + 2 * xh + j
                lane = 2 * w + co

                @pl.when((g != origin) | (p != lane))
                def _(a=a, j=j, w=w, origin=origin, lane=lane):
                    ref = grecv.at[a, j, w, :, 0:WIDTHS[w]]
                    copy(ref, ref, l5_s.at[0], l5_r.at[a, j, w], dev(origin, z * 4 + lane)).wait_recv()
    for k in range(3):
        load_state[k].wait()
        for i in range(1, 4):
            other = (p + i) % 4
            copy(state.at[k, other], state.at[k, other], st_s.at[k, i - 1], st_r.at[k, other], at_plane(other)).wait_recv()

    parts = [
        jnp.concatenate(
            [grecv[a, j, w, :, 0:WIDTHS[w]].astype(F32) for j in range(2) for w in range(2)], axis=1
        )
        for a in range(2)
    ]
    gradient = parts[0] + parts[1]
    old_master, old_first, old_second = [
        jnp.concatenate([state[k, q] for q in range(4)], axis=0) for k in range(3)
    ]
    m = first_decay * old_first + (1.0 - first_decay) * gradient
    v = second_decay * old_second + (1.0 - second_decay) * gradient * gradient
    w_new = old_master - learning_rate * (m / (jnp.sqrt(v / second_correction) + adam_epsilon))
    wtile[...] = w_new.astype(BF16)
    for k in range(1, NG):
        copy(wtile, wbuf.at[g], w2_s.at[k - 1], w2_r.at[g], dev((g + k) % NG, t)).start()
    wbuf[g] = wtile[...]
    for k, value in enumerate((w_new, m, v)):
        for q in range(4):
            newstate[k, q] = value[2 * q:2 * q + 2]
    results = (new_master, new_first, new_second)

    def back(k, i):
        other = (p + i) % 4
        return copy(
            newstate.at[k, other], results[k].at[:, quarter_cols(p)], back_s.at[k, i - 1], back_r.at[k, p], at_plane(other)
        )

    keep = [
        pltpu.make_async_copy(newstate.at[k, p], results[k].at[:, quarter_cols(p)], back_r.at[k, p]) for k in range(3)
    ]
    for k in range(3):
        for i in range(1, 4):
            back(k, i).start()
        keep[k].start()

    ring_step(4)
    ring_step(5)
    ring_step(6)
    ring_step(7)

    expand = jnp.where(
        lax.broadcasted_iota(jnp.int32, (ROWS // PAGE, ROWS), 1) // PAGE
        == lax.broadcasted_iota(jnp.int32, (ROWS // PAGE, ROWS), 0),
        1.0, 0.0,
    ).astype(BF16)
    load_stale.wait()
    load_old.wait()
    marks = jnp.broadcast_to(stale_v[...].astype(F32), (8, ROWS // PAGE)).astype(BF16)
    mask = jnp.dot(marks, expand, preferred_element_type=F32)[0:1]

    for k in range(1, NG):
        other = (g + k) % NG
        copy(wtile, wbuf.at[other], w2_s.at[k - 1], w2_r.at[other], dev(other, t)).wait_recv()
    reorder = select_matrix((PLANE_CH, PLANE_CH), lambda c: ((c % 32) // 2) * 8 + (c // 32) * 2 + c % 2)
    weights = jnp.dot(
        reorder, wbuf[...].astype(F32).reshape(PLANE_CH, QUARTER).astype(BF16), preferred_element_type=F32
    ).astype(BF16)

    ring_step(8)

    for k in range(6):
        rows = slice(256 * k, 256 * (k + 1))
        block = nbuf[...].reshape(ROWS, QUARTER)[rows]
        obuf[:, :, :, rows] = lax.dot_general(
            weights, block, (((1,), (1,)), ((), ())), preferred_element_type=F32
        ).reshape(2, 2, 32, 256)

    def o1_copy(k):
        return copy(obuf.at[k, 1 - co], o1.at[k], o1_s.at[k], o1_r.at[k], sibling)

    o1_copy(1 - xh).start()
    o1_copy(xh).start()
    o1_copy(1 - xh).wait_recv()
    o2send[...] = (obuf[1 - xh, co] + o1[1 - xh]).astype(BF16)
    o2_out = copy(o2send, o2, o2_s, o2_r, partner)
    o2_out.start()
    o1_copy(xh).wait_recv()
    osum[...] = obuf[xh, co] + o1[xh]
    o2_out.wait_recv()
    result = (osum[...] + o2[...].astype(F32)).astype(BF16)
    cache[0] = jnp.where(mask > 0.5, result, old_v[0])

    for k in range(3):
        keep[k].wait()
        for i in range(1, 4):
            other = (p + i) % 4
            copy(
                newstate.at[k, p], results[k].at[:, quarter_cols(other)], back_s.at[k, i - 1], back_r.at[k, other],
                at_plane(other),
            ).wait_recv()
            back(k, i).wait_send()
            st(k, i).wait_send()
    core_out.wait_send()
    x_out.wait_send()
    for w in range(2):
        pl.when(p != lane_of[w])(cot_out(w).wait_send)
    for step in range(8):
        for chunk in range(2):
            for d in range(2):
                if step < steps(d, chunk):
                    ring(d, step, chunk).wait_send()
    for j in range(4):
        for w in range(2):
            pl.when(l1_cond(j, w))(l1(j, w).wait_send)
    for w in range(2):
        @pl.when(is_lane[w])
        def _(w=w):
            for k in range(3):
                l2(k, w).wait_send()
            for k in range(4):
                l3(k, w, False).wait_send()
            for k in range(NG):
                pl.when((g != k) | (p != holder))(l5(k, w).wait_send)
    for k in range(1, NG):
        copy(wtile, wbuf.at[g], w2_s.at[k - 1], w2_r.at[g], dev((g + k) % NG, t)).wait_send()
    o1_copy(1 - xh).wait_send()
    o1_copy(xh).wait_send()
    o2_out.wait_send()


def local(hidden, norm_gain, cotangent, master, first_moment, second_moment, old_cache, stale_pages):
    dma = pltpu.SemaphoreType.DMA
    vmem = pl.BlockSpec(memory_space=pltpu.VMEM)
    hbm = pl.BlockSpec(memory_space=pl.ANY)
    state = jax.ShapeDtypeStruct((2, D), F32)
    scratch = [
        pltpu.VMEM((1, DEV_ROWS, D), BF16),
        pltpu.VMEM((1, D), F32),
        pltpu.VMEM((1, 32, ROWS), BF16),
        pltpu.VMEM((1, ROWS // PAGE), jnp.int32),
        pltpu.VMEM((2, 32, HALF), BF16),
        pltpu.VMEM((2, 32, HALF), BF16),
        pltpu.VMEM((2, CHIP_ROWS, QUARTER), BF16),
        pltpu.VMEM((NZ, 2, CHIP_ROWS, QUARTER), BF16),
        pltpu.VMEM((NZ, 2, CHIP_ROWS, WIDTHS[0]), BF16),
        pltpu.VMEM((4, 32, ROWS), BF16),
        pltpu.VMEM((PLANE_CH, ROWS), BF16),
        pltpu.VMEM((NG, 8, WIDTHS[0]), BF16),
        pltpu.VMEM((2, 2, 2, 8, WIDTHS[0]), BF16),
        pltpu.VMEM((3, 4, 2, QUARTER), F32),
        pltpu.VMEM((3, 4, 2, QUARTER), F32),
        pltpu.VMEM((8, QUARTER), BF16),
        pltpu.VMEM((NG, 8, QUARTER), BF16),
        pltpu.VMEM((2, 2, 32, ROWS), F32),
        pltpu.VMEM((2, 32, ROWS), F32),
        pltpu.VMEM((32, ROWS), F32),
        pltpu.VMEM((32, ROWS), BF16),
        pltpu.VMEM((32, ROWS), BF16),
        dma((4,)), dma, dma, dma, dma, dma((2, 8, 2)), dma((2, 8, 2)), dma((2,)), dma((4,)),
        dma((3, 3)), dma((3, 4)), dma((4, 2)), dma,
        dma((3,)), dma((3,)), dma((4,)), dma((4,)),
        dma((NG,)), dma((2, 2, 2)), dma((3, 3)), dma((3, 4)), dma((NG - 1,)), dma((NG,)),
        dma((2,)), dma((2,)), dma, dma,
    ]
    return pl.pallas_call(
        kernel,
        out_shape=(state, state, state, jax.ShapeDtypeStruct(old_cache.shape, BF16)),
        in_specs=[hbm] * 8,
        out_specs=(vmem,) * 4,
        scratch_shapes=scratch,
        compiler_params=pltpu.CompilerParams(
            collective_id=0, has_side_effects=True, vmem_limit_bytes=56 * 1024 * 1024
        ),
        cost_estimate=pl.CostEstimate(flops=800_000_000, bytes_accessed=2_000_000, transcendentals=20_000),
    )(
        hidden, norm_gain.reshape(1, D), cotangent, master, first_moment, second_moment, old_cache, stale_pages
    )


def solution(mesh):
    placed = (
        P("group", "tensor", None),
        P(),
        P("tensor", None),
        P(("tensor", "group"), None),
        P(("tensor", "group"), None),
        P(("tensor", "group"), None),
        P("group", "tensor", None),
        P("group", None),
    )
    return jax.shard_map(
        local,
        mesh=mesh,
        in_specs=placed,
        out_specs=(
            P(("tensor", "group"), None),
            P(("tensor", "group"), None),
            P(("tensor", "group"), None),
            P("group", "tensor", None),
        ),
        check_vma=False,
    )
```

```python
import jax
import jax.numpy as jnp
from jax import lax
from jax.experimental import pallas as pl
from jax.experimental.pallas import tpu as pltpu
from jax.sharding import PartitionSpec as P

PAGE = 16
D = 5120
ROWS = 1536
NZ = 16
NG = 16
DEV_ROWS = 24
CHIP_ROWS = 48
HALF = D // 2
QUARTER = D // 4
SLICE = D // 8
WIDTHS = (384, 256)
PLANE_CH = 128

learning_rate = 0.003
first_decay = 0.9
second_decay = 0.999
adam_epsilon = 1e-08
norm_epsilon = 1e-06
second_correction = 0.632304575229

MESH = pl.DeviceIdType.MESH
F32 = jnp.float32
BF16 = jnp.bfloat16


def select_matrix(shape, source_of_row):
    row = lax.broadcasted_iota(jnp.int32, shape, 0)
    col = lax.broadcasted_iota(jnp.int32, shape, 1)
    return jnp.where(col == source_of_row(row), 1.0, 0.0).astype(BF16)


def kernel(
    hidden, gain, cot, master, first, second, old, stale,
    new_state, cache,
    hidden_v, gain_v, old_v, stale_v, nsend, ncore, nmine, nbuf, n0, cots, cotp, gsend, grecv, state, newstate,
    wtile, wbuf, wmat, oall, opart, orecv, joined,
    in_s, core_s, core_r, x_s, x_r, ring_s, ring_r, cot_s, cot_r, st_s, st_r, l1_s, l1_r, l2_s, l2_r, l3_s, l3_r,
    l5_s, l5_r, back_s, back_r, w2_s, w2_r, o_s, o_r,
):
    g = lax.axis_index("group")
    t = lax.axis_index("tensor")
    xl = g // 8
    y = g % 8
    z = t // 4
    p = t % 4
    xh = p // 2
    co = p % 2

    def dev(group, tensor):
        return (group, tensor)

    def at_z(offset):
        return dev(g, ((z + offset + NZ) % NZ) * 4 + p)

    def at_plane(other):
        return dev(g, z * 4 + other)

    sibling = at_plane(2 * xh + (1 - co))
    across = 2 * (1 - xh) + co
    partner = at_plane(across)

    def copy(src, dst, ss, rs, where):
        return pltpu.make_async_remote_copy(
            src_ref=src, dst_ref=dst, send_sem=ss, recv_sem=rs, device_id=where, device_id_type=MESH
        )

    def quarter_cols(q):
        return pl.ds(pl.multiple_of((2 * (q % 2) + q // 2) * QUARTER, QUARTER), QUARTER)

    lane_of = [2 * w + y // 4 for w in range(2)]
    is_lane = [p == lane_of[w] for w in range(2)]
    any_lane = co == y // 4

    load_hidden = pltpu.make_async_copy(hidden, hidden_v, in_s.at[0])
    load_gain = pltpu.make_async_copy(gain, gain_v, in_s.at[1])
    load_old = pltpu.make_async_copy(old, old_v, in_s.at[2])
    load_stale = pltpu.make_async_copy(stale, stale_v, in_s.at[3])
    load_cot = pltpu.make_async_copy(cot, cots.at[p], cot_r.at[p])
    load_hidden.start()
    load_gain.start()
    load_old.start()
    load_stale.start()
    pl.when(any_lane)(load_cot.start)
    states = (master, first, second)
    load_state = [pltpu.make_async_copy(states[k].at[:, quarter_cols(p)], state.at[k, p], st_r.at[k, p]) for k in range(3)]
    for load in load_state:
        load.start()

    barrier = pltpu.get_barrier_semaphore()
    greet = [at_z(o) for o in (1, -1, 2, -2, 4, -4, 8)]
    greet += [at_plane((p + k) % 4) for k in (1, 2, 3)]
    greet += [dev((g + k) % NG, t) for k in range(1, NG)]
    greet += [dev((g + k) % NG, z * 4 + across) for k in range(1, NG)]
    for where in greet:
        pl.semaphore_signal(barrier, inc=1, device_id=where, device_id_type=MESH)

    load_hidden.wait()
    load_gain.wait()
    values = hidden_v[0].astype(F32)
    inverse = lax.rsqrt(jnp.mean(values * values, axis=-1, keepdims=True) + norm_epsilon)
    normed = (values * inverse * gain_v[...]).astype(BF16)
    for h in range(2):
        nsend[h, 0:DEV_ROWS] = normed[:, h * HALF:(h + 1) * HALF]
        nsend[h, DEV_ROWS:32] = jnp.zeros((8, HALF), BF16)
    ncore[co] = nsend[co]

    pl.semaphore_wait(barrier, len(greet))

    core_out = copy(nsend.at[1 - co], ncore.at[co], core_s, core_r, sibling)
    core_out.start()

    core_in = copy(nsend.at[1 - co], ncore.at[1 - co], core_s, core_r, sibling)
    core_in.wait_recv()
    for s in range(2):
        for c in range(2):
            nmine[s, c * DEV_ROWS:(c + 1) * DEV_ROWS] = ncore[c, 0:DEV_ROWS, s * QUARTER:(s + 1) * QUARTER]

    def ring(direction, step, chunk):
        sign = 1 if direction == 0 else -1
        slot = (z - sign * step + NZ) % NZ
        row = xh if chunk == 0 else 1 - xh
        src = nbuf.at[slot, row]
        if step == 0 and chunk == 0:
            src = nmine.at[xh]
        return copy(
            src, nbuf.at[slot, row], ring_s.at[direction, step, chunk], ring_r.at[direction, step, chunk],
            at_z(sign),
        )

    def ring_in(direction, step, chunk):
        sign = 1 if direction == 0 else -1
        slot = (z - sign * (step + 1) + NZ) % NZ
        row = xh if chunk == 0 else 1 - xh
        return copy(
            nbuf.at[slot, row], nbuf.at[slot, row], ring_s.at[direction, step, chunk],
            ring_r.at[direction, step, chunk], at_z(-sign),
        )

    def steps(direction, chunk):
        return 8 if direction == chunk else 7

    def l1(j, w):
        target = 8 * xh + 4 * co + j
        start = (j % 2) * SLICE + w * WIDTHS[0]
        return copy(
            nmine.at[j // 2, :, start:start + WIDTHS[w]], n0.at[z, xh, :, 0:WIDTHS[w]],
            l1_s.at[j, w], l1_r, dev(target, z * 4 + 2 * w + co),
        )

    def l1_cond(j, w):
        return (g == 0) & (p != 0) if (j, w) == (0, 0) else g == 0

    for j in range(4):
        for w in range(2):
            pl.when(l1_cond(j, w))(l1(j, w).start)
    x_out = copy(nmine.at[1 - xh], nbuf.at[z, xh], x_s, x_r, partner)
    x_out.start()
    for d in range(2):
        ring(d, 0, 0).start()

    def st(k, i):
        other = (p + i) % 4
        return copy(states[k].at[:, quarter_cols(other)], state.at[k, p], st_s.at[k, i - 1], st_r.at[k, p], at_plane(other))

    def cot_out(w):
        return copy(cot, cots.at[p], cot_s.at[w], cot_r.at[p], at_plane(lane_of[w]))

    @pl.when((g == 0) & (p == 0))
    def _():
        n0[z, 0] = nmine[0, :, 0:WIDTHS[0]]

    nbuf[z, xh] = nmine[xh]

    @pl.when(any_lane)
    def _():
        for k in range(NZ):
            n0[k, 1 - xl] = jnp.zeros((CHIP_ROWS, WIDTHS[0]), BF16)

    @pl.when(is_lane[1])
    def _():
        for k in range(NZ):
            n0[k, xl, :, WIDTHS[1]:WIDTHS[0]] = jnp.zeros((CHIP_ROWS, WIDTHS[0] - WIDTHS[1]), BF16)

    copy(nmine.at[xh], nbuf.at[z, 1 - xh], x_s, x_r, partner).wait_recv()
    for d in range(2):
        ring(d, 0, 1).start()

    for w in range(2):
        pl.when(p != lane_of[w])(cot_out(w).start)
    for i in range(1, 4):
        for k in range(3):
            st(k, i).start()

    def ring_step(step):
        for chunk in range(2):
            for d in range(2):
                if step - 1 < steps(d, chunk):
                    ring_in(d, step - 1, chunk).wait_recv()
                if step < steps(d, chunk):
                    ring(d, step, chunk).start()

    def l2(k, w):
        ref = n0.at[z, xl, :, 0:WIDTHS[w]]
        return copy(ref, ref, l2_s.at[k], l2_r.at[k], at_z(4 * (k + 1)))

    def l2_in(k, w):
        ref = n0.at[(z - 4 * (k + 1) + NZ) % NZ, xl, :, 0:WIDTHS[w]]
        return copy(ref, ref, l2_s.at[k], l2_r.at[k], at_z(-4 * (k + 1)))

    n0q = n0.reshape(4, 4, 2, CHIP_ROWS, WIDTHS[0])
    hops = ((1, 0, 4), (-1, 0, 4), (2, 0, 2), (-2, 2, 2))

    def l3(k, w, arriving):
        offset, start, size = hops[k]
        b = (z - offset + NZ) % 4 if arriving else z % 4
        ref = n0q.at[start:start + size, b, xl, :, 0:WIDTHS[w]]
        return copy(ref, ref, l3_s.at[k], l3_r.at[k], at_z(-offset if arriving else offset))

    for w in range(2):
        @pl.when(is_lane[w])
        def _(w=w):
            @pl.when((g != 0) | (p != 0))
            def _():
                ref = n0.at[z, xl, :, 0:WIDTHS[w]]
                copy(ref, ref, l1_s.at[0, 0], l1_r, dev((g + 1) % NG, t)).wait_recv()
            for k in range(3):
                l2(k, w).start()

    @pl.when(any_lane)
    def _():
        load_cot.wait()
        for k in range(1, 4):
            other = (p + k) % 4
            copy(cot, cots.at[other], cot_s.at[0], cot_r.at[other], at_plane(other)).wait_recv()
        order = select_matrix((PLANE_CH, PLANE_CH), lambda i: ((i // 2) % 4) * 32 + (i // 8) * 2 + i % 2)
        cotp[...] = jnp.dot(
            order, cots[...].reshape(PLANE_CH, ROWS), preferred_element_type=F32
        ).astype(BF16)

    ring_step(1)

    for w in range(2):
        @pl.when(is_lane[w])
        def _(w=w):
            for k in range(3):
                l2_in(k, w).wait_recv()
            for k in range(4):
                l3(k, w, False).start()

    ring_step(2)

    holder = 2 * ((y // 2) % 2) + y // 4

    def l5(k, w):
        return copy(
            gsend.at[k, :, 0:WIDTHS[w]], grecv.at[xl, y % 2, w, :, 0:WIDTHS[w]],
            l5_s.at[k], l5_r.at[xl, y % 2, w], dev(k, z * 4 + holder),
        )

    for w in range(2):
        @pl.when(is_lane[w])
        def _(w=w):
            for k in range(4):
                l3(k, w, True).wait_recv()

    @pl.when(any_lane)
    def _():
        gsend[...] = jnp.dot(
            cotp[...], n0[...].reshape(ROWS, WIDTHS[0]), preferred_element_type=F32
        ).reshape(NG, 8, WIDTHS[0]).astype(BF16)

    for w in range(2):
        @pl.when(is_lane[w])
        def _(w=w):
            for k in range(NG):
                pl.when((g != k) | (p != holder))(l5(k, w).start)

            @pl.when(p == holder)
            def _():
                grecv[xl, y % 2, w] = gsend[g]

    ring_step(3)

    for a in range(2):
        for j in range(2):
            for w in range(2):
                origin = 8 * a + 4 * co + 2 * xh + j
                lane = 2 * w + co

                @pl.when((g != origin) | (p != lane))
                def _(a=a, j=j, w=w, origin=origin, lane=lane):
                    ref = grecv.at[a, j, w, :, 0:WIDTHS[w]]
                    copy(ref, ref, l5_s.at[0], l5_r.at[a, j, w], dev(origin, z * 4 + lane)).wait_recv()
    for k in range(3):
        load_state[k].wait()
        for i in range(1, 4):
            other = (p + i) % 4
            copy(state.at[k, other], state.at[k, other], st_s.at[k, i - 1], st_r.at[k, other], at_plane(other)).wait_recv()

    parts = [
        jnp.concatenate(
            [grecv[a, j, w, :, 0:WIDTHS[w]].astype(F32) for j in range(2) for w in range(2)], axis=1
        )
        for a in range(2)
    ]
    gradient = parts[0] + parts[1]
    old_master, old_first, old_second = [
        jnp.concatenate([state[k, q] for q in range(4)], axis=0) for k in range(3)
    ]
    m = first_decay * old_first + (1.0 - first_decay) * gradient
    v = second_decay * old_second + (1.0 - second_decay) * gradient * gradient
    w_new = old_master - learning_rate * (m / (jnp.sqrt(v / second_correction) + adam_epsilon))
    wtile[...] = w_new.astype(BF16)
    for k in range(1, NG):
        copy(wtile, wbuf.at[g], w2_s.at[k - 1], w2_r.at[g], dev((g + k) % NG, t)).start()
    wbuf[g] = wtile[...]
    for k, value in enumerate((w_new, m, v)):
        for q in range(4):
            newstate[k, q] = value[2 * q:2 * q + 2]
    results = [new_state.at[k] for k in range(3)]

    def back(k, i):
        other = (p + i) % 4
        return copy(
            newstate.at[k, other], results[k].at[:, quarter_cols(p)], back_s.at[k, i - 1], back_r.at[k, p], at_plane(other)
        )

    keep = [
        pltpu.make_async_copy(newstate.at[k, p], results[k].at[:, quarter_cols(p)], back_r.at[k, p]) for k in range(3)
    ]
    for k in range(3):
        for i in range(1, 4):
            back(k, i).start()
        keep[k].start()

    ring_step(4)
    ring_step(5)

    expand = jnp.where(
        lax.broadcasted_iota(jnp.int32, (ROWS // PAGE, ROWS), 1) // PAGE
        == lax.broadcasted_iota(jnp.int32, (ROWS // PAGE, ROWS), 0),
        1.0, 0.0,
    ).astype(BF16)
    load_stale.wait()
    load_old.wait()
    marks = jnp.broadcast_to(stale_v[...].astype(F32), (8, ROWS // PAGE)).astype(BF16)
    mask = jnp.dot(marks, expand, preferred_element_type=F32)[0:1]

    ring_step(6)

    for k in range(1, NG):
        other = (g + k) % NG
        copy(wtile, wbuf.at[other], w2_s.at[k - 1], w2_r.at[other], dev(other, t)).wait_recv()
    reorder = select_matrix((PLANE_CH, PLANE_CH), lambda c: ((c % 32) // 2) * 8 + (c // 32) * 2 + c % 2)
    wmat[...] = jnp.dot(
        reorder, wbuf[...].astype(F32).reshape(PLANE_CH, QUARTER).astype(BF16), preferred_element_type=F32
    ).astype(BF16)

    def o_copy(slot, i):
        other = (p + i) % 4
        return copy(opart.at[slot, other], orecv.at[p, slot], o_s.at[i - 1, slot], o_r.at[p, slot], at_plane(other))

    def product(offset):
        slot = (z + offset + NZ) % NZ
        out = lax.dot_general(
            wmat[...], nbuf[slot].reshape(2 * CHIP_ROWS, QUARTER), (((1,), (1,)), ((), ())), preferred_element_type=F32
        ).reshape(4, 32, 2 * CHIP_ROWS)
        oall[slot] = out
        opart[slot] = out.astype(BF16)
        for i in range(1, 4):
            o_copy(slot, i).start()

    def products(first_offset, count):
        def body(i, carry):
            product(first_offset + i)
            return carry

        lax.fori_loop(0, count, body, 0)

    products(-3, 7)
    ring_step(7)
    products(-7, 4)
    products(4, 4)

    for k in range(3):
        keep[k].wait()
        for i in range(1, 4):
            other = (p + i) % 4
            copy(
                newstate.at[k, p], results[k].at[:, quarter_cols(other)], back_s.at[k, i - 1], back_r.at[k, other],
                at_plane(other),
            ).wait_recv()
            back(k, i).wait_send()
            st(k, i).wait_send()
    core_out.wait_send()
    x_out.wait_send()
    for w in range(2):
        pl.when(p != lane_of[w])(cot_out(w).wait_send)
    for j in range(4):
        for w in range(2):
            pl.when(l1_cond(j, w))(l1(j, w).wait_send)
    for w in range(2):
        @pl.when(is_lane[w])
        def _(w=w):
            for k in range(3):
                l2(k, w).wait_send()
            for k in range(4):
                l3(k, w, False).wait_send()
            for k in range(NG):
                pl.when((g != k) | (p != holder))(l5(k, w).wait_send)
    for k in range(1, NG):
        copy(wtile, wbuf.at[g], w2_s.at[k - 1], w2_r.at[g], dev((g + k) % NG, t)).wait_send()

    def ring_sent(step):
        for chunk in range(2):
            for d in range(2):
                if step < steps(d, chunk):
                    ring(d, step, chunk).wait_send()

    for step in range(7):
        ring_sent(step)

    ring_step(8)
    product(8)
    ring_sent(7)

    for slot in range(NZ):
        part = oall[slot, p]
        for i in range(1, 4):
            other = (p + i) % 4
            copy(
                opart.at[slot, p], orecv.at[other, slot], o_s.at[i - 1, slot], o_r.at[other, slot], at_plane(other)
            ).wait_recv()
            part = part + orecv[other, slot].astype(F32)
        joined[:, slot * 2 * CHIP_ROWS:(slot + 1) * 2 * CHIP_ROWS] = part
    cache[0] = jnp.where(mask > 0.5, joined[...].astype(BF16), old_v[0])

    for slot in range(NZ):
        for i in range(1, 4):
            o_copy(slot, i).wait_send()


def local(hidden, norm_gain, cotangent, master, first_moment, second_moment, old_cache, stale_pages):
    dma = pltpu.SemaphoreType.DMA
    vmem = pl.BlockSpec(memory_space=pltpu.VMEM)
    hbm = pl.BlockSpec(memory_space=pl.ANY)
    scratch = [
        pltpu.VMEM((1, DEV_ROWS, D), BF16),
        pltpu.VMEM((1, D), F32),
        pltpu.VMEM((1, 32, ROWS), BF16),
        pltpu.VMEM((1, ROWS // PAGE), jnp.int32),
        pltpu.VMEM((2, 32, HALF), BF16),
        pltpu.VMEM((2, 32, HALF), BF16),
        pltpu.VMEM((2, CHIP_ROWS, QUARTER), BF16),
        pltpu.VMEM((NZ, 2, CHIP_ROWS, QUARTER), BF16),
        pltpu.VMEM((NZ, 2, CHIP_ROWS, WIDTHS[0]), BF16),
        pltpu.VMEM((4, 32, ROWS), BF16),
        pltpu.VMEM((PLANE_CH, ROWS), BF16),
        pltpu.VMEM((NG, 8, WIDTHS[0]), BF16),
        pltpu.VMEM((2, 2, 2, 8, WIDTHS[0]), BF16),
        pltpu.VMEM((3, 4, 2, QUARTER), F32),
        pltpu.VMEM((3, 4, 2, QUARTER), F32),
        pltpu.VMEM((8, QUARTER), BF16),
        pltpu.VMEM((NG, 8, QUARTER), BF16),
        pltpu.VMEM((PLANE_CH, QUARTER), BF16),
        pltpu.VMEM((NZ, 4, 32, 2 * CHIP_ROWS), F32),
        pltpu.VMEM((NZ, 4, 32, 2 * CHIP_ROWS), BF16),
        pltpu.VMEM((4, NZ, 32, 2 * CHIP_ROWS), BF16),
        pltpu.VMEM((32, ROWS), F32),
        dma((4,)), dma, dma, dma, dma, dma((2, 8, 2)), dma((2, 8, 2)), dma((2,)), dma((4,)),
        dma((3, 3)), dma((3, 4)), dma((4, 2)), dma,
        dma((3,)), dma((3,)), dma((4,)), dma((4,)),
        dma((NG,)), dma((2, 2, 2)), dma((3, 3)), dma((3, 4)), dma((NG - 1,)), dma((NG,)),
        dma((3, NZ)), dma((4, NZ)),
    ]
    new_state, cache = pl.pallas_call(
        kernel,
        out_shape=(jax.ShapeDtypeStruct((3, 2, D), F32), jax.ShapeDtypeStruct(old_cache.shape, BF16)),
        in_specs=[hbm] * 8,
        out_specs=(vmem,) * 2,
        scratch_shapes=scratch,
        compiler_params=pltpu.CompilerParams(
            collective_id=0, has_side_effects=True, vmem_limit_bytes=56 * 1024 * 1024
        ),
        cost_estimate=pl.CostEstimate(flops=800_000_000, bytes_accessed=2_000_000, transcendentals=20_000),
    )(
        hidden, norm_gain.reshape(1, D), cotangent, master, first_moment, second_moment, old_cache, stale_pages
    )
    return new_state[0], new_state[1], new_state[2], cache


def solution(mesh):
    placed = (
        P("group", "tensor", None),
        P(),
        P("tensor", None),
        P(("tensor", "group"), None),
        P(("tensor", "group"), None),
        P(("tensor", "group"), None),
        P("group", "tensor", None),
        P("group", None),
    )
    return jax.shard_map(
        local,
        mesh=mesh,
        in_specs=placed,
        out_specs=(
            P(("tensor", "group"), None),
            P(("tensor", "group"), None),
            P(("tensor", "group"), None),
            P("group", "tensor", None),
        ),
        check_vma=False,
    )
```

```python
import jax
import jax.numpy as jnp
from jax import lax
from jax.experimental import pallas as pl
from jax.experimental.pallas import tpu as pltpu
from jax.sharding import PartitionSpec as P

PAGE = 16
D = 5120
ROWS = 1536
NZ = 16
NG = 16
DEV_ROWS = 24
CHIP_ROWS = 48
HALF = D // 2
QUARTER = D // 4
SLICE = D // 8
WIDTHS = (384, 256)
PLANE_CH = 128

learning_rate = 0.003
first_decay = 0.9
second_decay = 0.999
adam_epsilon = 1e-08
norm_epsilon = 1e-06
second_correction = 0.632304575229

MESH = pl.DeviceIdType.MESH
F32 = jnp.float32
BF16 = jnp.bfloat16


def select_matrix(shape, source_of_row):
    row = lax.broadcasted_iota(jnp.int32, shape, 0)
    col = lax.broadcasted_iota(jnp.int32, shape, 1)
    return jnp.where(col == source_of_row(row), 1.0, 0.0).astype(BF16)


def kernel(
    hidden, gain, cot, master, first, second, old, stale,
    new_state, cache,
    hidden_v, gain_v, old_v, stale_v, nsend, ncore, nmine, nbuf, n0, cots, cotp, gsend, grecv, state, newstate,
    wtile, wbuf, wmat, oall, opart, orecv, joined,
    in_s, core_s, core_r, x_s, x_r, begin_s, begin_r, ring_s, ring_r, cot_s, cot_r, st_s, st_r, l1_s, l1_r, l2_s, l2_r, l3_s, l3_r,
    l5_s, l5_r, back_s, back_r, w2_s, w2_r, o_s, o_r,
):
    g = lax.axis_index("group")
    t = lax.axis_index("tensor")
    xl = g // 8
    y = g % 8
    z = t // 4
    p = t % 4
    xh = p // 2
    co = p % 2

    def dev(group, tensor):
        return (group, tensor)

    def at_z(offset):
        return dev(g, ((z + offset + NZ) % NZ) * 4 + p)

    def at_plane(other):
        return dev(g, z * 4 + other)

    sibling = at_plane(2 * xh + (1 - co))
    across = 2 * (1 - xh) + co
    partner = at_plane(across)

    def copy(src, dst, ss, rs, where):
        return pltpu.make_async_remote_copy(
            src_ref=src, dst_ref=dst, send_sem=ss, recv_sem=rs, device_id=where, device_id_type=MESH
        )

    def quarter_cols(q):
        return pl.ds(pl.multiple_of((2 * (q % 2) + q // 2) * QUARTER, QUARTER), QUARTER)

    lane_of = [2 * w + y // 4 for w in range(2)]
    is_lane = [p == lane_of[w] for w in range(2)]
    any_lane = co == y // 4

    load_hidden = pltpu.make_async_copy(hidden, hidden_v, in_s.at[0])
    load_gain = pltpu.make_async_copy(gain, gain_v, in_s.at[1])
    load_old = pltpu.make_async_copy(old, old_v, in_s.at[2])
    load_stale = pltpu.make_async_copy(stale, stale_v, in_s.at[3])
    load_cot = pltpu.make_async_copy(cot, cots.at[p], cot_r.at[p])
    load_hidden.start()
    load_gain.start()
    load_old.start()
    load_stale.start()
    pl.when(any_lane)(load_cot.start)
    states = (master, first, second)
    load_state = [pltpu.make_async_copy(states[k].at[:, quarter_cols(p)], state.at[k, p], st_r.at[k, p]) for k in range(3)]
    for load in load_state:
        load.start()

    barrier = pltpu.get_barrier_semaphore()
    greet = [at_z(o) for o in (1, -1, 2, -2, 4, -4, 8)]
    greet += [at_plane((p + k) % 4) for k in (1, 2, 3)]
    greet += [dev((g + k) % NG, t) for k in range(1, NG)]
    greet += [dev((g + k) % NG, z * 4 + across) for k in range(1, NG)]
    for where in greet:
        pl.semaphore_signal(barrier, inc=1, device_id=where, device_id_type=MESH)

    load_hidden.wait()
    load_gain.wait()
    values = hidden_v[0].astype(F32)
    inverse = lax.rsqrt(jnp.mean(values * values, axis=-1, keepdims=True) + norm_epsilon)
    normed = (values * inverse * gain_v[...]).astype(BF16)
    for h in range(2):
        nsend[h, 0:DEV_ROWS] = normed[:, h * HALF:(h + 1) * HALF]
        nsend[h, DEV_ROWS:32] = jnp.zeros((8, HALF), BF16)
    ncore[co] = nsend[co]

    pl.semaphore_wait(barrier, len(greet))

    core_out = copy(nsend.at[1 - co], ncore.at[co], core_s, core_r, sibling)
    core_out.start()

    core_in = copy(nsend.at[1 - co], ncore.at[1 - co], core_s, core_r, sibling)
    core_in.wait_recv()
    for s in range(2):
        for c in range(2):
            nmine[s, c * DEV_ROWS:(c + 1) * DEV_ROWS] = ncore[c, 0:DEV_ROWS, s * QUARTER:(s + 1) * QUARTER]

    def ring(direction, step, chunk):
        sign = 1 if direction == 0 else -1
        slot = (z - sign * step + NZ) % NZ
        row = xh if chunk == 0 else 1 - xh
        src = nbuf.at[slot, row]
        if step == 0 and chunk == 0:
            src = nmine.at[xh]
        return copy(
            src, nbuf.at[slot, row], ring_s.at[direction, step, chunk], ring_r.at[direction, step, chunk],
            at_z(sign),
        )

    def ring_in(direction, step, chunk):
        sign = 1 if direction == 0 else -1
        slot = (z - sign * (step + 1) + NZ) % NZ
        row = xh if chunk == 0 else 1 - xh
        return copy(
            nbuf.at[slot, row], nbuf.at[slot, row], ring_s.at[direction, step, chunk],
            ring_r.at[direction, step, chunk], at_z(-sign),
        )

    def steps(direction, chunk):
        return 8 if direction == chunk else 7

    def l1(j, w):
        target = 8 * xh + 4 * co + j
        start = (j % 2) * SLICE + w * WIDTHS[0]
        return copy(
            nmine.at[j // 2, :, start:start + WIDTHS[w]], n0.at[z, xh, :, 0:WIDTHS[w]],
            l1_s.at[j, w], l1_r, dev(target, z * 4 + 2 * w + co),
        )

    def l1_cond(j, w):
        return (g == 0) & (p != 0) if (j, w) == (0, 0) else g == 0

    for j in range(4):
        for w in range(2):
            pl.when(l1_cond(j, w))(l1(j, w).start)
    pieces = (slice(0, 32), slice(32, CHIP_ROWS))

    def x_out(h):
        return copy(
            nmine.at[1 - xh, pieces[h]], nbuf.at[z, xh, pieces[h]], x_s.at[h], x_r.at[h], partner
        )

    for h in range(2):
        x_out(h).start()
    for d in range(2):
        ring(d, 0, 0).start()

    def st(k, i):
        other = (p + i) % 4
        return copy(states[k].at[:, quarter_cols(other)], state.at[k, p], st_s.at[k, i - 1], st_r.at[k, p], at_plane(other))

    def cot_out(w):
        return copy(cot, cots.at[p], cot_s.at[w], cot_r.at[p], at_plane(lane_of[w]))

    @pl.when((g == 0) & (p == 0))
    def _():
        n0[z, 0] = nmine[0, :, 0:WIDTHS[0]]

    nbuf[z, xh] = nmine[xh]

    @pl.when(any_lane)
    def _():
        for k in range(NZ):
            n0[k, 1 - xl] = jnp.zeros((CHIP_ROWS, WIDTHS[0]), BF16)

    @pl.when(is_lane[1])
    def _():
        for k in range(NZ):
            n0[k, xl, :, WIDTHS[1]:WIDTHS[0]] = jnp.zeros((CHIP_ROWS, WIDTHS[0] - WIDTHS[1]), BF16)

    def begin(d, h, arriving):
        sign = 1 if d == 0 else -1
        slot = (z - sign + NZ) % NZ if arriving else z
        ref = nbuf.at[slot, 1 - xh, pieces[h]]
        return copy(ref, ref, begin_s.at[d, h], begin_r.at[d, h], at_z(-sign if arriving else sign))

    for h in range(2):
        ref = nbuf.at[z, 1 - xh, pieces[h]]
        copy(ref, ref, x_s.at[h], x_r.at[h], partner).wait_recv()
        for d in range(2):
            begin(d, h, False).start()

    for w in range(2):
        pl.when(p != lane_of[w])(cot_out(w).start)
    for i in range(1, 4):
        for k in range(3):
            st(k, i).start()

    def ring_step(step):
        for chunk in range(2):
            for d in range(2):
                if step == 1 and chunk == 1:
                    for h in range(2):
                        begin(d, h, True).wait_recv()
                elif step - 1 < steps(d, chunk):
                    ring_in(d, step - 1, chunk).wait_recv()
                if step < steps(d, chunk):
                    ring(d, step, chunk).start()

    def l2(k, w):
        ref = n0.at[z, xl, :, 0:WIDTHS[w]]
        return copy(ref, ref, l2_s.at[k], l2_r.at[k], at_z(4 * (k + 1)))

    def l2_in(k, w):
        ref = n0.at[(z - 4 * (k + 1) + NZ) % NZ, xl, :, 0:WIDTHS[w]]
        return copy(ref, ref, l2_s.at[k], l2_r.at[k], at_z(-4 * (k + 1)))

    n0q = n0.reshape(4, 4, 2, CHIP_ROWS, WIDTHS[0])
    hops = ((1, 0, 4), (-1, 0, 4), (2, 0, 2), (-2, 2, 2))

    def l3(k, w, arriving):
        offset, start, size = hops[k]
        b = (z - offset + NZ) % 4 if arriving else z % 4
        ref = n0q.at[start:start + size, b, xl, :, 0:WIDTHS[w]]
        return copy(ref, ref, l3_s.at[k], l3_r.at[k], at_z(-offset if arriving else offset))

    for w in range(2):
        @pl.when(is_lane[w])
        def _(w=w):
            @pl.when((g != 0) | (p != 0))
            def _():
                ref = n0.at[z, xl, :, 0:WIDTHS[w]]
                copy(ref, ref, l1_s.at[0, 0], l1_r, dev((g + 1) % NG, t)).wait_recv()
            for k in range(3):
                l2(k, w).start()

    @pl.when(any_lane)
    def _():
        load_cot.wait()
        for k in range(1, 4):
            other = (p + k) % 4
            copy(cot, cots.at[other], cot_s.at[0], cot_r.at[other], at_plane(other)).wait_recv()
        order = select_matrix((PLANE_CH, PLANE_CH), lambda i: ((i // 2) % 4) * 32 + (i // 8) * 2 + i % 2)
        cotp[...] = jnp.dot(
            order, cots[...].reshape(PLANE_CH, ROWS), preferred_element_type=F32
        ).astype(BF16)

    ring_step(1)

    for w in range(2):
        @pl.when(is_lane[w])
        def _(w=w):
            for k in range(3):
                l2_in(k, w).wait_recv()
            for k in range(4):
                l3(k, w, False).start()

    ring_step(2)

    holder = 2 * ((y // 2) % 2) + y // 4

    def l5(k, w):
        return copy(
            gsend.at[k, :, 0:WIDTHS[w]], grecv.at[xl, y % 2, w, :, 0:WIDTHS[w]],
            l5_s.at[k], l5_r.at[xl, y % 2, w], dev(k, z * 4 + holder),
        )

    for w in range(2):
        @pl.when(is_lane[w])
        def _(w=w):
            for k in range(4):
                l3(k, w, True).wait_recv()

    @pl.when(any_lane)
    def _():
        gsend[...] = jnp.dot(
            cotp[...], n0[...].reshape(ROWS, WIDTHS[0]), preferred_element_type=F32
        ).reshape(NG, 8, WIDTHS[0]).astype(BF16)

    for w in range(2):
        @pl.when(is_lane[w])
        def _(w=w):
            for k in range(NG):
                pl.when((g != k) | (p != holder))(l5(k, w).start)

            @pl.when(p == holder)
            def _():
                grecv[xl, y % 2, w] = gsend[g]

    ring_step(3)

    for a in range(2):
        for j in range(2):
            for w in range(2):
                origin = 8 * a + 4 * co + 2 * xh + j
                lane = 2 * w + co

                @pl.when((g != origin) | (p != lane))
                def _(a=a, j=j, w=w, origin=origin, lane=lane):
                    ref = grecv.at[a, j, w, :, 0:WIDTHS[w]]
                    copy(ref, ref, l5_s.at[0], l5_r.at[a, j, w], dev(origin, z * 4 + lane)).wait_recv()
    for k in range(3):
        load_state[k].wait()
        for i in range(1, 4):
            other = (p + i) % 4
            copy(state.at[k, other], state.at[k, other], st_s.at[k, i - 1], st_r.at[k, other], at_plane(other)).wait_recv()

    parts = [
        jnp.concatenate(
            [grecv[a, j, w, :, 0:WIDTHS[w]].astype(F32) for j in range(2) for w in range(2)], axis=1
        )
        for a in range(2)
    ]
    gradient = parts[0] + parts[1]
    old_master, old_first, old_second = [
        jnp.concatenate([state[k, q] for q in range(4)], axis=0) for k in range(3)
    ]
    m = first_decay * old_first + (1.0 - first_decay) * gradient
    v = second_decay * old_second + (1.0 - second_decay) * gradient * gradient
    w_new = old_master - learning_rate * (m / (jnp.sqrt(v / second_correction) + adam_epsilon))
    wtile[...] = w_new.astype(BF16)
    for k in range(1, NG):
        copy(wtile, wbuf.at[g], w2_s.at[k - 1], w2_r.at[g], dev((g + k) % NG, t)).start()
    wbuf[g] = wtile[...]
    for k, value in enumerate((w_new, m, v)):
        for q in range(4):
            newstate[k, q] = value[2 * q:2 * q + 2]
    results = [new_state.at[k] for k in range(3)]

    def back(k, i):
        other = (p + i) % 4
        return copy(
            newstate.at[k, other], results[k].at[:, quarter_cols(p)], back_s.at[k, i - 1], back_r.at[k, p], at_plane(other)
        )

    keep = [
        pltpu.make_async_copy(newstate.at[k, p], results[k].at[:, quarter_cols(p)], back_r.at[k, p]) for k in range(3)
    ]
    for k in range(3):
        for i in range(1, 4):
            back(k, i).start()
        keep[k].start()

    ring_step(4)
    ring_step(5)

    expand = jnp.where(
        lax.broadcasted_iota(jnp.int32, (ROWS // PAGE, ROWS), 1) // PAGE
        == lax.broadcasted_iota(jnp.int32, (ROWS // PAGE, ROWS), 0),
        1.0, 0.0,
    ).astype(BF16)
    load_stale.wait()
    load_old.wait()
    marks = jnp.broadcast_to(stale_v[...].astype(F32), (8, ROWS // PAGE)).astype(BF16)
    mask = jnp.dot(marks, expand, preferred_element_type=F32)[0:1]

    ring_step(6)

    for k in range(1, NG):
        other = (g + k) % NG
        copy(wtile, wbuf.at[other], w2_s.at[k - 1], w2_r.at[other], dev(other, t)).wait_recv()
    reorder = select_matrix((PLANE_CH, PLANE_CH), lambda c: ((c % 32) // 2) * 8 + (c // 32) * 2 + c % 2)
    wmat[...] = jnp.dot(
        reorder, wbuf[...].astype(F32).reshape(PLANE_CH, QUARTER).astype(BF16), preferred_element_type=F32
    ).astype(BF16)

    def o_copy(slot, i):
        other = (p + i) % 4
        return copy(opart.at[slot, other], orecv.at[p, slot], o_s.at[i - 1, slot], o_r.at[p, slot], at_plane(other))

    def product(offset):
        slot = (z + offset + NZ) % NZ
        out = lax.dot_general(
            wmat[...], nbuf[slot].reshape(2 * CHIP_ROWS, QUARTER), (((1,), (1,)), ((), ())), preferred_element_type=F32
        ).reshape(4, 32, 2 * CHIP_ROWS)
        oall[slot] = out
        opart[slot] = out.astype(BF16)
        for i in range(1, 4):
            o_copy(slot, i).start()

    def products(first_offset, count):
        def body(i, carry):
            product(first_offset + i)
            return carry

        lax.fori_loop(0, count, body, 0)

    def collect(offset):
        slot = (z + offset + NZ) % NZ
        part = oall[slot, p]
        for i in range(1, 4):
            other = (p + i) % 4
            copy(
                opart.at[slot, p], orecv.at[other, slot], o_s.at[i - 1, slot], o_r.at[other, slot], at_plane(other)
            ).wait_recv()
            part = part + orecv[other, slot].astype(F32)
        oall[slot, p] = part
        for i in range(1, 4):
            o_copy(slot, i).wait_send()

    def collect_all(first_offset, count):
        def body(i, carry):
            collect(first_offset + i)
            return carry

        lax.fori_loop(0, count, body, 0)

    products(-5, 11)
    ring_step(7)
    products(-7, 2)
    products(6, 2)

    for k in range(3):
        keep[k].wait()
        for i in range(1, 4):
            other = (p + i) % 4
            copy(
                newstate.at[k, p], results[k].at[:, quarter_cols(other)], back_s.at[k, i - 1], back_r.at[k, other],
                at_plane(other),
            ).wait_recv()
            back(k, i).wait_send()
            st(k, i).wait_send()
    core_out.wait_send()
    for h in range(2):
        x_out(h).wait_send()
    for w in range(2):
        pl.when(p != lane_of[w])(cot_out(w).wait_send)
    for j in range(4):
        for w in range(2):
            pl.when(l1_cond(j, w))(l1(j, w).wait_send)
    for w in range(2):
        @pl.when(is_lane[w])
        def _(w=w):
            for k in range(3):
                l2(k, w).wait_send()
            for k in range(4):
                l3(k, w, False).wait_send()
            for k in range(NG):
                pl.when((g != k) | (p != holder))(l5(k, w).wait_send)
    for k in range(1, NG):
        copy(wtile, wbuf.at[g], w2_s.at[k - 1], w2_r.at[g], dev((g + k) % NG, t)).wait_send()

    def ring_sent(step):
        for chunk in range(2):
            for d in range(2):
                if step == 0 and chunk == 1:
                    for h in range(2):
                        begin(d, h, False).wait_send()
                elif step < steps(d, chunk):
                    ring(d, step, chunk).wait_send()

    for step in range(7):
        ring_sent(step)

    collect_all(-5, 11)

    ring_step(8)
    product(8)
    ring_sent(7)
    collect_all(-7, 2)
    collect_all(6, 3)
    for slot in range(NZ):
        joined[:, slot * 2 * CHIP_ROWS:(slot + 1) * 2 * CHIP_ROWS] = oall[slot, p]
    cache[0] = jnp.where(mask > 0.5, joined[...].astype(BF16), old_v[0])


def local(hidden, norm_gain, cotangent, master, first_moment, second_moment, old_cache, stale_pages):
    dma = pltpu.SemaphoreType.DMA
    vmem = pl.BlockSpec(memory_space=pltpu.VMEM)
    hbm = pl.BlockSpec(memory_space=pl.ANY)
    scratch = [
        pltpu.VMEM((1, DEV_ROWS, D), BF16),
        pltpu.VMEM((1, D), F32),
        pltpu.VMEM((1, 32, ROWS), BF16),
        pltpu.VMEM((1, ROWS // PAGE), jnp.int32),
        pltpu.VMEM((2, 32, HALF), BF16),
        pltpu.VMEM((2, 32, HALF), BF16),
        pltpu.VMEM((2, CHIP_ROWS, QUARTER), BF16),
        pltpu.VMEM((NZ, 2, CHIP_ROWS, QUARTER), BF16),
        pltpu.VMEM((NZ, 2, CHIP_ROWS, WIDTHS[0]), BF16),
        pltpu.VMEM((4, 32, ROWS), BF16),
        pltpu.VMEM((PLANE_CH, ROWS), BF16),
        pltpu.VMEM((NG, 8, WIDTHS[0]), BF16),
        pltpu.VMEM((2, 2, 2, 8, WIDTHS[0]), BF16),
        pltpu.VMEM((3, 4, 2, QUARTER), F32),
        pltpu.VMEM((3, 4, 2, QUARTER), F32),
        pltpu.VMEM((8, QUARTER), BF16),
        pltpu.VMEM((NG, 8, QUARTER), BF16),
        pltpu.VMEM((PLANE_CH, QUARTER), BF16),
        pltpu.VMEM((NZ, 4, 32, 2 * CHIP_ROWS), F32),
        pltpu.VMEM((NZ, 4, 32, 2 * CHIP_ROWS), BF16),
        pltpu.VMEM((4, NZ, 32, 2 * CHIP_ROWS), BF16),
        pltpu.VMEM((32, ROWS), F32),
        dma((4,)), dma, dma, dma((2,)), dma((2,)), dma((2, 2)), dma((2, 2)), dma((2, 8, 2)), dma((2, 8, 2)), dma((2,)), dma((4,)),
        dma((3, 3)), dma((3, 4)), dma((4, 2)), dma,
        dma((3,)), dma((3,)), dma((4,)), dma((4,)),
        dma((NG,)), dma((2, 2, 2)), dma((3, 3)), dma((3, 4)), dma((NG - 1,)), dma((NG,)),
        dma((3, NZ)), dma((4, NZ)),
    ]
    new_state, cache = pl.pallas_call(
        kernel,
        out_shape=(jax.ShapeDtypeStruct((3, 2, D), F32), jax.ShapeDtypeStruct(old_cache.shape, BF16)),
        in_specs=[hbm] * 8,
        out_specs=(vmem,) * 2,
        scratch_shapes=scratch,
        compiler_params=pltpu.CompilerParams(
            collective_id=0, has_side_effects=True, vmem_limit_bytes=56 * 1024 * 1024
        ),
        cost_estimate=pl.CostEstimate(flops=800_000_000, bytes_accessed=2_000_000, transcendentals=20_000),
    )(
        hidden, norm_gain.reshape(1, D), cotangent, master, first_moment, second_moment, old_cache, stale_pages
    )
    return new_state[0], new_state[1], new_state[2], cache


def solution(mesh):
    placed = (
        P("group", "tensor", None),
        P(),
        P("tensor", None),
        P(("tensor", "group"), None),
        P(("tensor", "group"), None),
        P(("tensor", "group"), None),
        P("group", "tensor", None),
        P("group", None),
    )
    return jax.shard_map(
        local,
        mesh=mesh,
        in_specs=placed,
        out_specs=(
            P(("tensor", "group"), None),
            P(("tensor", "group"), None),
            P(("tensor", "group"), None),
            P("group", "tensor", None),
        ),
        check_vma=False,
    )
```
